128 devices in a mesh: dp: 32 (over x, y_lo, z), code: 4 (over y_hi, core).
Axes of the slice: x: 4, y: 4 (y_hi: 2, y_lo: 2; y = y_hi * 2 + y_lo), z: 4, core: 2. Of those that a mesh axis runs over, the one named last changes fastest.
Arguments:
- grads: bfloat16 [32, 4, 512, 16384], P('dp', 'code'), may hold values from -1.59375 to 1.59375
- master: float32 [4, 512, 16384], P('code', 'dp'), may hold values from -6 to 6
- moment_one: float32 [4, 512, 16384], P('code', 'dp'), may hold values from -3 to 3
- moment_two: float32 [4, 512, 16384], P('code', 'dp'), may hold values from 0.05 to 1
- generator: float32 [4, 16], replicated, may hold values from 0.5 to 2
- member_slot: int32 [32, 4], P('dp', 'code'), may hold values from 0 to 15, as said below
- holder: int32 [32, 4], replicated, may hold values from 0 to 15, as said below
Outputs:
- updated: float32 [4, 512, 16384], P('code', 'dp')
- new_one: float32 [4, 512, 16384], P('code', 'dp')
- new_two: float32 [4, 512, 16384], P('code', 'dp')
- parity: float32 [4, 128, 16384], P('code', 'dp')
The draws below stay inside these ranges and needn't reach their ends.
Inputs may be any that keep to these rules, and one draw needn't show every extreme that they name: `member_slot`: within each coding group (the devices whose dp index has the same remainder modulo 8), the 16 devices have 16 different slots. `holder`: within each coding group, the 16 devices hold 16 different blocks.
All inputs are finite; a program needn't handle non-finite values.
Results may differ from the reference program's by a relative error of at most 0.0003.
Values sent between devices are 32-bit elements; how exact they have to be, the bound alone decides.
A program may use at most 128 MiB of HBM per device.

```python
import math
import jax
import jax.numpy as jnp
from jax import lax

D = 16384
RD = 16
GROUP = 16
PARITIES = 4
STRIDE = 8
RQ = 4
N_DP = 32
N_CODE = 4


def group_layout(key):
    keys = jax.random.split(key, STRIDE)
    orders = jax.vmap(lambda single: jax.random.permutation(single, 16))(keys)
    grid = orders.reshape(STRIDE, 4, 4)
    return jnp.transpose(grid, (1, 0, 2)).reshape(N_DP, N_CODE).astype(jnp.int32)


def draw_member_slot(key, part):
    key = jax.random.fold_in(key, 3)
    return group_layout(key)


def draw_holder(key, part):
    key = jax.random.fold_in(key, 7)
    return group_layout(key)


def raised(result, stream_key, source, target, shards_of, factor):
    def block_of(axis_at):
        return (jnp.arange(result.shape[axis_at]) // (result.shape[axis_at] // shards_of)).reshape((-1,) + (1,) * (result.ndim - 1 - axis_at))

    one_side = jax.random.permutation(stream_key, shards_of)[block_of(target)]
    other_side = (block_of(target) + shards_of // 2) % shards_of
    return jnp.where((block_of(source) == one_side) | (block_of(source) == other_side), factor * result, result)


def block_levels(own_key, extent, pieces, low, top_value):
    def one(axis_at, blocks):
        heights = jax.random.uniform(jax.random.fold_in(jax.random.fold_in(own_key, 6), axis_at), (blocks,), jnp.float32, low / len(pieces), top_value / len(pieces))
        return jnp.repeat(jnp.exp(heights), extent[axis_at] // blocks).reshape((-1,) + (1,) * (len(extent) - axis_at - 1))

    level = one(*pieces[0])
    for cut in pieces[1:]:
        level = level * one(*cut)
    return level


def bell_draw(rng, shape, spread, reach, cuts=(), dtype=jnp.bfloat16):
    level = block_levels(rng, shape, cuts, -0.22, 0.18) if cuts else 1.0
    values = jax.random.normal(rng, shape, jnp.float32) * spread * level
    return jnp.minimum(jnp.maximum(values, -reach), reach).astype(dtype)


def bell_draw_with(stream_key, shape, spread, bound, cuts, heavy, dtype=jnp.bfloat16):
    entries = spread * jax.random.normal(stream_key, shape, jnp.float32)
    if cuts:
        entries = entries * block_levels(stream_key, shape, cuts, -0.22, 0.18)
    return jnp.clip(raised(entries, jax.random.fold_in(stream_key, 3), *heavy), -bound, bound).astype(dtype)


def setup_inputs(seed: int = 0) -> dict:
    arg_keys = jax.random.split(jax.random.key(seed), 8)
    return {
        "grads": bell_draw_with(arg_keys[0], (N_DP, N_CODE, N_DP * RD, D), 0.2, 1.59375, ((0, 32), (1, 4)), (0, 2, 32, 2.75)),
        "master": bell_draw(arg_keys[1], (N_CODE, N_DP * RD, D), 1.0, 6.0, ((0, 4), (1, 32)), jnp.float32),
        "moment_one": bell_draw(arg_keys[2], (N_CODE, N_DP * RD, D), 0.5, 3.0, ((0, 4), (1, 32)), jnp.float32),
        "moment_two": jnp.clip(jnp.exp(math.log(1.0) - 2.9957323 * jax.random.uniform(arg_keys[3], (N_CODE, N_DP * RD, D), jnp.float32) ** block_levels(arg_keys[3], (N_CODE, N_DP * RD, D), ((0, 4), (1, 32)), -0.2, 0.2)), 0.05, 1.0),
        "generator": jnp.clip(jax.random.uniform(arg_keys[4], (PARITIES, GROUP), jnp.float32, 0.5, 2.0), 0.5, 2.0),
        "member_slot": draw_member_slot(jax.random.fold_in(arg_keys[7], 71), 0),
        "holder": draw_holder(jax.random.fold_in(arg_keys[7], 71), 0),
    }


beta_one = 0.9
beta_two = 0.999
learn_rate = 0.05
decay_rate = 0.1
epsilon = 1e-08
correct_one = 1.0 - 0.9 ** 10
correct_two = 1.0 - 0.999 ** 10

def reference(grads, master, moment_one, moment_two, generator, member_slot, holder):

    def accumulate(total, piece):
        return (total + piece.astype(jnp.float32), None)
    summed, unused = lax.scan(accumulate, jnp.zeros(grads.shape[1:], jnp.float32), grads)
    new_one = beta_one * moment_one + (1.0 - beta_one) * summed
    new_two = beta_two * moment_two + (1.0 - beta_two) * summed * summed
    direction = new_one / correct_one / (jnp.sqrt(new_two / correct_two) + epsilon)
    updated = master - learn_rate * (direction + decay_rate * master)
    stacked = updated.reshape(N_CODE, 4, STRIDE, RD, D)
    slot_grid = member_slot.reshape(4, STRIDE, N_CODE)
    coefficients = jnp.transpose(generator[:, slot_grid], (0, 3, 1, 2))
    full = jnp.einsum('pcab,cabrd->bprd', coefficients, stacked, precision=lax.Precision.HIGHEST)
    blocks = full.reshape(STRIDE, PARITIES * 4, RQ, D)
    dest_group = (jnp.arange(N_DP) % STRIDE).astype(jnp.int32)
    picked = blocks[dest_group[None, :], jnp.transpose(holder)]
    parity = picked.reshape(N_CODE, N_DP * RQ, D)
    return (updated, new_one, new_two, parity)
```

```python
import functools

import jax
import jax.numpy as jnp
from jax import lax
from jax.experimental import pallas as pl
from jax.experimental.pallas import tpu as pltpu
from jax.sharding import PartitionSpec as P

MESH = pl.DeviceIdType.MESH

beta_one = 0.9
beta_two = 0.999
learn_rate = 0.05
decay_rate = 0.1
epsilon = 1e-08
correct_one = 1.0 - 0.9**10
correct_two = 1.0 - 0.999**10

D = 16384
X, Z, Y = range(3)
XP, XM, X2, ZP, ZM, Z2, YN, YH, CORE, XPH, XMH, X2H = range(12)
AXES = {X: ((XP, XM, X2), (ZP, ZM, Z2)), Z: ((ZP, ZM, Z2), (XP, XM, X2)), Y: ((ZP, ZM, Z2), (XP, XM, X2))}
WIDE = {X: 384, Z: 256, Y: 384}
WIDE_STEPS = 14
NARROW = {X: 128, Z: 128, Y: 256}
NARROW_STEPS = 4
WIDE_COLS, NARROW_COLS = sum(WIDE.values()), sum(NARROW.values())
GRAD_SLOTS = 5
SLOTS = 3
PLACE = {(2, 0): 0, (1, 1): 1, (2, 1): 2, (3, 0): 3, (1, 0): 4, (3, 1): 5, (0, 0): 6, (0, 1): 7}

assert WIDE_COLS * WIDE_STEPS + NARROW_COLS * NARROW_STEPS == D


class Scratch:
    def __init__(self, pool, spec):
        self.spec, self.ref = spec, None
        pool.append(self)


class Copy:
    def __init__(self, pool, to, src, dst, slots, steps):
        self.to, self.src, self.dst, self.slots = to, src, dst, slots
        self.send = Scratch(pool, pltpu.SemaphoreType.DMA((slots,)))
        self.recv = Scratch(pool, pltpu.SemaphoreType.DMA((steps,)))

    def at(self, c, where):
        slot = lax.rem(c, self.slots)
        return pltpu.make_async_remote_copy(
            src_ref=self.src(slot, c),
            dst_ref=self.dst(c),
            send_sem=self.send.ref.at[slot],
            recv_sem=self.recv.ref.at[c],
            device_id=where[self.to],
            device_id_type=MESH,
        )


class Ring:
    def __init__(self, pool, axis, steps, rows, cols, staged):
        self.came = [Scratch(pool, pltpu.VMEM((steps, 2, rows, cols), jnp.float32)) for _ in range(2)]
        self.passed = Scratch(pool, pltpu.VMEM((steps, 2, rows, cols), jnp.float32))
        self.copies, self.on = [], []
        if staged:
            self.staged = [Scratch(pool, pltpu.VMEM((SLOTS, 2, rows, cols), jnp.float32)) for _ in range(2)]
        else:
            self.acc = Scratch(pool, pltpu.VMEM((SLOTS, 8, rows, cols), jnp.float32))
        for way in range(2):

            def first(slot, c, way=way):
                return self.staged[way].ref.at[slot] if staged else self.acc.ref.at[slot, pl.ds(2 * way, 2)]

            def landed(c, way=way):
                return self.came[way].ref.at[c]

            def second(slot, c, way=way):
                return self.came[way].ref.at[c, 0]

            def last(c, way=way):
                return self.passed.ref.at[c, way]

            self.copies.append(Copy(pool, axis[way], first, landed, SLOTS, steps))
            self.on.append(Copy(pool, axis[way], second, last, SLOTS, steps))


class Direct:
    def __init__(self, pool, axis, steps, rows, cols):
        self.acc = Scratch(pool, pltpu.VMEM((steps, 4, rows, cols), jnp.float32))
        self.came = Scratch(pool, pltpu.VMEM((steps, 3, rows, cols), jnp.float32))
        self.copies = []
        for k, to in ((1, axis[0]), (2, axis[2]), (3, axis[1])):

            def src(slot, c, k=k):
                return self.acc.ref.at[c, k]

            def dst(c, k=k):
                return self.came.ref.at[c, k - 1]

            self.copies.append(Copy(pool, to, src, dst, steps, steps))


class Fan:
    def __init__(self, pool, steps, rows, cols):
        self.acc = Scratch(pool, pltpu.VMEM((steps, 8, rows, cols), jnp.float32))
        self.came = Scratch(pool, pltpu.VMEM((steps, 8, rows, cols), jnp.float32))
        self.copies = {}
        for at, to in ((1, YH), (2, XP), (3, XPH), (4, X2), (5, X2H), (6, XM), (7, XMH)):

            def src(slot, c, at=at):
                return self.acc.ref.at[c, at]

            def dst(c, at=at):
                return self.came.ref.at[c, at]

            self.copies[at] = Copy(pool, to, src, dst, steps, steps)


class Swap:
    def __init__(self, pool, to, steps, slots, shape):
        self.out = Scratch(pool, pltpu.VMEM((slots, *shape), jnp.float32))
        self.own = Scratch(pool, pltpu.VMEM((slots, *shape), jnp.float32))
        self.came = Scratch(pool, pltpu.VMEM((steps, *shape), jnp.float32))
        self.copy = Copy(
            pool, to, lambda slot, c: self.out.ref.at[slot], lambda c: self.came.ref.at[c], slots, steps
        )


class Side:
    def __init__(self, pool, to, steps, slots, shape):
        self.out = Scratch(pool, pltpu.VMEM((slots, *shape), jnp.float32))
        self.came = Scratch(pool, pltpu.VMEM((steps, *shape), jnp.float32))
        self.copy = Copy(
            pool, to, lambda slot, c: self.out.ref.at[slot], lambda c: self.came.ref.at[c], slots, steps
        )


class Steps:
    def __init__(self, pool, widths, steps, first_column, slots, grad_slots):
        self.widths, self.steps, self.first_column = widths, steps, first_column
        self.cols = sum(widths.values())
        self.start = {X: 0, Z: widths[X], Y: widths[X] + widths[Z]}
        self.slots, self.grad_slots = slots, grad_slots
        self.grad = Scratch(pool, pltpu.VMEM((grad_slots, 512, self.cols), jnp.bfloat16))
        self.grad_sem = Scratch(pool, pltpu.SemaphoreType.DMA((grad_slots,)))
        self.out_sem = Scratch(pool, pltpu.SemaphoreType.DMA((3, slots)))
        self.swap = {t: Swap(pool, YN, steps, slots, (16, widths[t])) for t in (X, Z)}
        self.side = Side(pool, YN, steps, slots, (4, 64, widths[Y]))
        self.core = Swap(pool, CORE, steps, slots, (32, self.cols))

    def columns(self, c, offset=0, width=None):
        return pl.ds(
            pl.multiple_of(self.first_column + c * self.cols + offset, 128), self.cols if width is None else width
        )


def plan():
    pool = []
    state = [Scratch(pool, pltpu.VMEM((16, D), jnp.float32)) for _ in range(3)]
    state_sem = Scratch(pool, pltpu.SemaphoreType.DMA((3,)))
    select = Scratch(pool, pltpu.VMEM((64, 16), jnp.float32))
    wide = Steps(pool, WIDE, WIDE_STEPS, 0, SLOTS, GRAD_SLOTS)
    n = WIDE_STEPS
    wide.level = {
        t: [
            Ring(pool, AXES[t][0], n, 32 if t == Y else 64, WIDE[t], t != Y),
            Ring(pool, AXES[t][1], n, 8 if t == Y else 16, WIDE[t], False),
        ]
        for t in (X, Z, Y)
    }
    wide.yh = Swap(pool, YH, n, SLOTS, (8, WIDE_COLS // 2))
    wide.parity = Ring(pool, AXES[X][0], n, 8, WIDE_COLS // 2, False)
    n = NARROW_STEPS
    narrow = Steps(pool, NARROW, n, WIDE_STEPS * WIDE_COLS, n, n)
    narrow.level = {
        t: [
            Direct(pool, AXES[t][0], n, 64 if t == Y else 128, NARROW[t]),
            Direct(pool, AXES[t][1], n, 16 if t == Y else 32, NARROW[t]),
        ]
        for t in (X, Z, Y)
    }
    narrow.parity = Fan(pool, n, 8, NARROW_COLS // 2)
    return pool, state, state_sem, select, wide, narrow


def kernel(planned, grads, master, one, two, generator, member_slot, holder, *rest):
    pool, state, state_sem, select, wide, narrow = planned
    outs, parity = rest[:3], rest[3]
    for made, ref in zip(pool, rest[4:], strict=True):
        made.ref = ref
    dp, code = lax.axis_index("dp"), lax.axis_index("code")
    x, yl, z = dp // 8, lax.rem(dp // 4, 2), lax.rem(dp, 4)
    yh, core = code // 2, lax.rem(code, 2)

    def device(x=x, yl=yl, z=z, yh=yh, core=core):
        return (x * 8 + yl * 4 + z, yh * 2 + core)

    def around(at, by):
        return lax.rem(at + by, 4)

    where = {
        XP: device(x=around(x, 1)),
        XM: device(x=around(x, 3)),
        X2: device(x=around(x, 2)),
        ZP: device(z=around(z, 1)),
        ZM: device(z=around(z, 3)),
        Z2: device(z=around(z, 2)),
        YN: device(yl=1 - yl),
        YH: device(yh=1 - yh),
        CORE: device(core=1 - core),
        XPH: device(x=around(x, 1), yh=1 - yh),
        XMH: device(x=around(x, 3), yh=1 - yh),
        X2H: device(x=around(x, 2), yh=1 - yh),
    }
    place = {X: (x, z), Z: (z, x), Y: (z, x)}

    def start(copy, c):
        copy.at(c, where).start()

    def arrive(*copies, c):
        for copy in copies:
            copy.at(c, where).wait_recv()

    def left(*copies, c):
        for copy in copies:
            copy.at(c, where).wait_send()

    def load(s, c):
        slot = lax.rem(c, s.grad_slots)
        return pltpu.make_async_copy(
            grads.at[0, 0, :, s.columns(c)], s.grad.ref.at[slot], s.grad_sem.ref.at[slot]
        )

    given = [
        pltpu.make_async_copy(ref.at[0], held.ref, state_sem.ref.at[at])
        for at, (ref, held) in enumerate(zip((master, one, two), state, strict=True))
    ]

    def store(s, at, c):
        columns = s.columns(c)
        return pltpu.make_async_copy(
            state[at].ref.at[:, columns],
            outs[at].at[0, :, columns],
            s.out_sem.ref.at[at, lax.rem(c, s.slots)],
        )

    def grad(s, t, c, row, rows):
        block = s.grad.ref[
            lax.rem(c, s.grad_slots), pl.ds(pl.multiple_of(row, 16), rows), pl.ds(s.start[t], s.widths[t])
        ]
        return block.astype(jnp.float32)

    def first_row(t, a, h, b):
        return (a * 128 + b * 16 if t == X else a * 16 + b * 128) + h * 64

    def own(s, t, c, a, h):
        if t == X:
            return [(0, 64, grad(s, t, c, first_row(t, a, h, 0), 64))]
        return [(16 * b, 16, grad(s, t, c, first_row(t, a, h, b), 16)) for b in range(4)]

    def fill_side(s, c):
        slot = lax.rem(c, s.slots)
        for b in range(4):
            s.side.out.ref[slot, b] = grad(s, Y, c, b * 128 + (1 - yl) * 64, 64)

    def side_block(s, c, at, b):
        mine = grad(s, Y, c, b * 128 + yl * 64 + at * 16, 16)
        return mine + s.side.came.ref[c, b, pl.ds(pl.multiple_of(at * 16, 16), 16)]

    def adam(s, t, c, summed):
        columns = s.columns(c, s.start[t], s.widths[t])
        held_master, held_one, held_two = (held.ref for held in state)
        weights = held_master[:, columns]
        new_one = beta_one * held_one[:, columns] + (1.0 - beta_one) * summed
        new_two = beta_two * held_two[:, columns] + (1.0 - beta_two) * summed * summed
        direction = new_one / correct_one / (jnp.sqrt(new_two / correct_two) + epsilon)
        held_master[:, columns] = weights - learn_rate * (direction + decay_rate * weights)
        held_one[:, columns] = new_one
        held_two[:, columns] = new_two

    def terms(s, c):
        slot = lax.rem(c, s.slots)
        updated = state[0].ref[:, s.columns(c)]

        def weighted(rows):
            return jnp.dot(
                select.ref[rows], updated, precision=lax.Precision.HIGHEST, preferred_element_type=jnp.float32
            )

        s.core.out.ref[slot] = weighted(pl.ds(32, 32))
        start(s.core.copy, c)
        for at in range(3):
            store(s, at, c).start()
        s.core.own.ref[slot] = weighted(pl.ds(0, 32))

    def end_swaps(s, c, halves):
        slot = lax.rem(c, s.slots)
        for t in (X, Z):
            arrive(s.swap[t].copy, c=c)
            adam(s, t, c, s.swap[t].own.ref[slot] + s.swap[t].came.ref[c])
        adam(s, Y, c, halves)
        terms(s, c)

    def start_swap(s, t, c, low, high):
        slot = lax.rem(c, s.slots)
        s.swap[t].out.ref[slot] = jnp.where(yl == 0, high, low)
        start(s.swap[t].copy, c)
        s.swap[t].own.ref[slot] = jnp.where(yl == 0, low, high)

    def write_parity(s, c, total):
        half = s.cols // 2
        for h in range(2):
            parity[0, :, s.columns(c, half * h, half)] = total[4 * h : 4 * h + 4]


    def pass_on(ring, c, mine):
        for way in range(2):
            arrive(ring.copies[way], c=c)
            for row, rows, value in mine(way):
                ring.came[way].ref[c, 0, pl.ds(row, rows)] += value
            start(ring.on[way], c)

    def held_part(ring, c):
        slot = lax.rem(c, SLOTS)
        rows = ring.acc.spec.shape[2]
        return lambda way: [(0, rows, ring.acc.ref[slot, 4 + way])]

    def grad_part(t, c):
        a = place[t][0]
        return lambda way: own(wide, t, c, around(a, (1, 3)[way]), way)

    def fill_eight(ring, c, block):
        slot = lax.rem(c, SLOTS)

        def put(k, h):
            ring.acc.ref[slot, PLACE[k, h]] = block(k, h)

        put(2, 0)
        put(1, 1)
        start(ring.copies[0], c)
        put(2, 1)
        put(3, 0)
        start(ring.copies[1], c)
        for k, h in ((1, 0), (3, 1), (0, 0), (0, 1)):
            put(k, h)

    def halves(ring, c):
        slot = lax.rem(c, SLOTS)
        arrive(*ring.on, c=c)
        return [
            ring.acc.ref[slot, 6 + h] + ring.came[1 - h].ref[c, 1] + ring.passed.ref[c, h] for h in range(2)
        ]

    def second_axis(t, c):
        slot = lax.rem(c, SLOTS)
        ring, after = wide.level[t]
        r = after.acc.spec.shape[2]
        at_a, at_b = place[t]
        arrive(*ring.on, c=c)

        def block(k, h):
            b = around(at_b, k)
            rows = pl.ds(pl.multiple_of(b * r, r), r)
            if t == Y:
                mine = ring.acc.ref[slot, 6 + h, rows]
            else:
                mine = grad(wide, t, c, first_row(t, at_a, h, b), 16)
            return mine + ring.came[1 - h].ref[c, 1, rows] + ring.passed.ref[c, h, rows]

        fill_eight(after, c, block)

    def fill_wide(c):
        slot = lax.rem(c, SLOTS)
        load(wide, c).wait()
        fill_side(wide, c)
        for t in (X, Z):
            ring, a = wide.level[t][0], place[t][0]
            for way, parts in enumerate((((2, 0), (1, 1)), ((2, 1), (3, 0)))):
                for at, (k, h) in enumerate(parts):
                    for row, rows, value in own(wide, t, c, around(a, k), h):
                        ring.staged[way].ref[slot, at, pl.ds(row, rows)] = value

    def wide0(c):
        start(wide.side.copy, c)
        for way in range(2):
            for t in (X, Z):
                start(wide.level[t][0].copies[way], c)

    def wide1(c):
        slot = lax.rem(c, SLOTS)
        for t in (X, Z):
            pass_on(wide.level[t][0], c, grad_part(t, c))
        arrive(wide.side.copy, c=c)
        ring = wide.level[Y][0]

        def block(k):
            at = around(z, k)
            for b in range(4):
                total = side_block(wide, c, at, b)
                for h in range(2):
                    ring.acc.ref[slot, PLACE[k, h], pl.ds(8 * b, 8)] = total[8 * h : 8 * h + 8]

        block(2)
        block(1)
        start(ring.copies[0], c)
        block(3)
        start(ring.copies[1], c)
        block(0)

    def wide2(c):
        left(*wide.level[X][0].copies, *wide.level[Z][0].copies, wide.side.copy, c=c)
        for t in (X, Z):
            second_axis(t, c)
        pass_on(wide.level[Y][0], c, held_part(wide.level[Y][0], c))

    def wide3(c):
        left(*wide.level[X][0].on, *wide.level[Z][0].on, *wide.level[Y][0].copies, c=c)
        for t in (X, Z):
            pass_on(wide.level[t][1], c, held_part(wide.level[t][1], c))
        second_axis(Y, c)

    def wide4(c):
        left(*wide.level[X][1].copies, *wide.level[Z][1].copies, *wide.level[Y][0].on, c=c)
        for t in (X, Z):
            start_swap(wide, t, c, *halves(wide.level[t][1], c))
        pass_on(wide.level[Y][1], c, held_part(wide.level[Y][1], c))

    def wide5(c):
        left(*wide.level[X][1].on, *wide.level[Z][1].on, *wide.level[Y][1].copies, c=c)

        @pl.when(c == 0)
        def _():
            for copy in given:
                copy.wait()

        end_swaps(wide, c, jnp.concatenate(halves(wide.level[Y][1], c), axis=0))

    def wide6(c):
        slot = lax.rem(c, SLOTS)
        left(wide.swap[X].copy, wide.swap[Z].copy, *wide.level[Y][1].on, c=c)
        arrive(wide.core.copy, c=c)
        half = WIDE_COLS // 2

        def block(k, h):
            rows, columns = pl.ds(8 * k, 8), pl.ds(half * h, half)
            return wide.core.own.ref[slot, rows, columns] + wide.core.came.ref[c, rows, columns]

        fill_eight(wide.parity, c, block)

    def wide7(c):
        left(wide.core.copy, c=c)
        pass_on(wide.parity, c, held_part(wide.parity, c))
        for at in range(3):
            store(wide, at, c).wait()

    def wide8(c):
        slot = lax.rem(c, SLOTS)
        left(*wide.parity.copies, c=c)
        low, high = halves(wide.parity, c)
        wide.yh.out.ref[slot] = jnp.concatenate([low[4:8], high[4:8]], axis=0)
        start(wide.yh.copy, c)
        wide.yh.own.ref[slot] = jnp.concatenate([low[0:4], high[0:4]], axis=0)

    def wide9(c):
        left(*wide.parity.on, c=c)
        arrive(wide.yh.copy, c=c)
        write_parity(wide, c, wide.yh.own.ref[lax.rem(c, SLOTS)] + wide.yh.came.ref[c])
        left(wide.yh.copy, c=c)


    def fill_four(level, c, block):
        for k in (2, 1, 3):
            block(k)
            start(level.copies[k - 1], c)
        block(0)

    def whole(level, c):
        arrive(*level.copies, c=c)
        acc, came = level.acc.ref, level.came.ref
        return (acc[c, 0] + came[c, 0]) + (came[c, 1] + came[c, 2])

    def fill_narrow(c):
        load(narrow, c).wait()
        fill_side(narrow, c)
        for t in (X, Z):
            for k in range(4):
                for h in range(2):
                    for row, rows, value in own(narrow, t, c, around(place[t][0], k), h):
                        narrow.level[t][0].acc.ref[c, k, pl.ds(64 * h + row, rows)] = value

    def narrow0(c):
        start(narrow.side.copy, c)
        for k in (2, 1, 3):
            for t in (X, Z):
                start(narrow.level[t][0].copies[k - 1], c)

    def narrow1(c):
        for t in (X, Z):
            level, after = narrow.level[t]
            arrive(*level.copies, c=c)

            def block(k, t=t, level=level, after=after):
                b = around(place[t][1], k)
                for h in range(2):
                    rows = pl.ds(pl.multiple_of(64 * h + 16 * b, 16), 16)
                    acc, came = level.acc.ref, level.came.ref
                    after.acc.ref[c, k, pl.ds(16 * h, 16)] = (acc[c, 0, rows] + came[c, 0, rows]) + (
                        came[c, 1, rows] + came[c, 2, rows]
                    )

            fill_four(after, c, block)
        arrive(narrow.side.copy, c=c)
        level = narrow.level[Y][0]

        def side(k):
            for b in range(4):
                level.acc.ref[c, k, pl.ds(16 * b, 16)] = side_block(narrow, c, around(z, k), b)

        fill_four(level, c, side)

    def narrow2(c):
        for t in (X, Z):
            both = whole(narrow.level[t][1], c)
            start_swap(narrow, t, c, both[0:16], both[16:32])
        level, after = narrow.level[Y]
        arrive(*level.copies, c=c)

        def block(k):
            rows = pl.ds(pl.multiple_of(16 * around(x, k), 16), 16)
            acc, came = level.acc.ref, level.came.ref
            after.acc.ref[c, k] = (acc[c, 0, rows] + came[c, 0, rows]) + (came[c, 1, rows] + came[c, 2, rows])

        fill_four(after, c, block)

    def narrow3(c):
        end_swaps(narrow, c, whole(narrow.level[Y][1], c))

    def narrow4(c):
        arrive(narrow.core.copy, c=c)
        fan, half = narrow.parity, NARROW_COLS // 2
        for k in (2, 1, 3, 0):
            rows = pl.ds(8 * k, 8)
            block = narrow.core.own.ref[c, rows] + narrow.core.came.ref[c, rows]
            for other in (1, 0):
                part = block[4 * other : 4 * other + 4]
                fan.acc.ref[c, 2 * k + other] = jnp.concatenate([part[:, 0:half], part[:, half:]], axis=0)
                if k or other:
                    start(fan.copies[2 * k + other], c)

    def narrow5(c):
        fan = narrow.parity
        arrive(*fan.copies.values(), c=c)
        total = fan.acc.ref[c, 0]
        for at in fan.copies:
            total += fan.came.ref[c, at]
        write_parity(narrow, c, total)
        for t in (X, Z):
            left(*narrow.level[t][0].copies, *narrow.level[t][1].copies, narrow.swap[t].copy, c=c)
        left(*narrow.level[Y][0].copies, *narrow.level[Y][1].copies, narrow.side.copy, c=c)
        left(narrow.core.copy, *fan.copies.values(), c=c)
        for at in range(3):
            store(narrow, at, c).wait()

    def selector():
        def iota(shape, dimension):
            return lax.broadcasted_iota(jnp.int32, shape, dimension)

        def parts(shape):
            row = iota(shape, 0)
            d = row // 4
            first = lax.rem(x + lax.rem(d // 2, 4), 4) * 8 + lax.rem(dp, 8)
            second = lax.rem(yh + lax.rem(d, 2), 2) * 2 + lax.rem(core + d // 8, 2)
            return first, second, lax.rem(row, 4).astype(jnp.float32)

        first, second, _ = parts((64, 32))
        held = holder[...].astype(jnp.float32)
        mask = first == iota((64, 32), 1)
        picked = jnp.zeros((64, 32), jnp.float32)
        for at in range(4):
            picked += jnp.where(mask & (second == at), held[at : at + 1, :], 0.0)
        block = jnp.sum(picked, axis=1, keepdims=True)
        lane = iota((64, 16), 1)
        lane_value = lane.astype(jnp.float32)
        hit = lane_value == block
        column = jnp.sum(
            jnp.where(iota((4, 16), 1) == member_slot[...], generator[...], 0.0), axis=1, keepdims=True
        )
        spread = jnp.sum(jnp.where(iota((4, 16), 0) == iota((4, 16), 1) // 4, column, 0.0), axis=0, keepdims=True)
        scale = jnp.sum(jnp.where(hit, spread, 0.0), axis=1, keepdims=True)
        quarter = jnp.sum(
            jnp.where(hit, lax.rem(lane, 4).astype(jnp.float32), 0.0), axis=1, keepdims=True
        )
        _, _, row_in = parts((64, 16))
        select.ref[...] = jnp.where(lane_value == quarter * 4.0 + row_in, scale, 0.0)

    barrier = pltpu.get_barrier_semaphore()
    for to in where.values():
        pl.semaphore_signal(barrier, inc=1, device_id=to, device_id_type=MESH)
    for c in range(GRAD_SLOTS - 2):
        load(wide, c).start()
    for copy in given:
        copy.start()
    for c in range(NARROW_STEPS):
        load(narrow, c).start()
    fill_wide(0)
    selector()
    pl.semaphore_wait(barrier, len(where))

    wide_stages = (wide0, wide1, wide2, wide3, wide4, wide5, wide6, wide7, wide8, wide9)
    narrow_stages = (narrow0, narrow1, narrow2, narrow3, narrow4, narrow5)
    last = max(WIDE_STEPS + len(wide_stages), WIDE_STEPS + NARROW_STEPS + len(narrow_stages)) - 1

    def step(t, carry):
        for lag in range(len(wide_stages)):

            @pl.when((t >= lag) & (t < WIDE_STEPS + lag))
            def _(lag=lag):
                wide_stages[lag](t - lag)

            if lag < len(narrow_stages):
                begin = WIDE_STEPS + lag

                @pl.when((t >= begin) & (t < begin + NARROW_STEPS))
                def _(lag=lag, begin=begin):
                    narrow_stages[lag](t - begin)

        @pl.when(t + 1 < WIDE_STEPS)
        def _():
            fill_wide(t + 1)

        @pl.when((t + 1 >= WIDE_STEPS) & (t + 1 < WIDE_STEPS + NARROW_STEPS))
        def _():
            fill_narrow(t + 1 - WIDE_STEPS)

        @pl.when(t + GRAD_SLOTS - 2 < WIDE_STEPS)
        def _():
            load(wide, t + GRAD_SLOTS - 2).start()

        return carry

    lax.fori_loop(0, last, step, 0)


def finish(count, *refs):
    given, outs, held = refs[:count], refs[count : 2 * count], refs[2 * count : 3 * count]
    sem = refs[3 * count]
    parts = []
    for at in range(count):
        pieces = 4 if given[at].shape[1] % 16 == 0 else 1
        columns = given[at].shape[2] // pieces
        for piece in range(pieces):
            part = (slice(None), slice(None), pl.ds(piece * columns, columns))
            parts.append(
                (
                    pltpu.make_async_copy(given[at].at[part], held[at].at[part], sem.at[0, at, piece]),
                    pltpu.make_async_copy(held[at].at[part], outs[at].at[part], sem.at[1, at, piece]),
                )
            )
    for read, _ in parts:
        read.start()
    for read, write in parts:
        read.wait()
        write.start()
    for _, write in parts:
        write.wait()


def shards(grads, master, moment_one, moment_two, generator, member_slot, holder):
    planned = plan()
    anywhere = pl.BlockSpec(memory_space=pl.ANY)
    vmem = pl.BlockSpec(memory_space=pltpu.VMEM)
    state = jax.ShapeDtypeStruct(master.shape, jnp.float32)
    made = (state, state, state, jax.ShapeDtypeStruct((1, 4, D), jnp.float32))
    results = pl.pallas_call(
        functools.partial(kernel, planned),
        out_shape=made,
        in_specs=[anywhere] * 4 + [vmem] * 3,
        out_specs=(anywhere, anywhere, anywhere, vmem),
        scratch_shapes=[part.spec for part in planned[0]],
        name="adam_parity",
        compiler_params=pltpu.CompilerParams(
            collective_id=0, has_side_effects=True, vmem_limit_bytes=63 * 2**20
        ),
    )(grads, master, moment_one, moment_two, generator, member_slot, holder.T)
    return pl.pallas_call(
        functools.partial(finish, 4),
        out_shape=made,
        in_specs=[anywhere] * 4,
        out_specs=(anywhere,) * 4,
        scratch_shapes=[pltpu.VMEM(part.shape, part.dtype) for part in made] + [pltpu.SemaphoreType.DMA((2, 4, 4))],
        name="write_out",
        compiler_params=pltpu.CompilerParams(vmem_limit_bytes=63 * 2**20),
    )(*results)


def solution(mesh):
    state = P("code", "dp", None)
    return jax.shard_map(
        shards,
        mesh=mesh,
        in_specs=(P("dp", "code", None, None), state, state, state, P(), P("dp", "code"), P()),
        out_specs=(state, state, state, state),
        check_vma=False,
    )
```

```python
import functools

import jax
import jax.numpy as jnp
from jax import lax
from jax.experimental import pallas as pl
from jax.experimental.pallas import tpu as pltpu
from jax.sharding import PartitionSpec as P

MESH = pl.DeviceIdType.MESH

beta_one = 0.9
beta_two = 0.999
learn_rate = 0.05
decay_rate = 0.1
epsilon = 1e-08
correct_one = 1.0 - 0.9**10
correct_two = 1.0 - 0.999**10

D = 16384
X, Z, Y = range(3)
XP, XM, X2, ZP, ZM, Z2, YN, YH, CORE, XPH, XMH, X2H = range(12)
AXES = {X: ((XP, XM, X2), (ZP, ZM, Z2)), Z: ((ZP, ZM, Z2), (XP, XM, X2)), Y: ((ZP, ZM, Z2), (XP, XM, X2))}
WIDE = {X: 384, Z: 256, Y: 384}
WIDE_STEPS = 15
NARROW = {X: 128, Z: 128, Y: 256}
NARROW_STEPS = 2
WIDE_COLS, NARROW_COLS = sum(WIDE.values()), sum(NARROW.values())
GRAD_SLOTS = 5
SLOTS = 3
PLACE = {(2, 0): 0, (1, 1): 1, (2, 1): 2, (3, 0): 3, (1, 0): 4, (3, 1): 5, (0, 0): 6, (0, 1): 7}

assert WIDE_COLS * WIDE_STEPS + NARROW_COLS * NARROW_STEPS == D


class Scratch:
    def __init__(self, pool, spec):
        self.spec, self.ref = spec, None
        pool.append(self)


class Copy:
    def __init__(self, pool, to, src, dst, slots, steps):
        self.to, self.src, self.dst, self.slots = to, src, dst, slots
        self.send = Scratch(pool, pltpu.SemaphoreType.DMA((slots,)))
        self.recv = Scratch(pool, pltpu.SemaphoreType.DMA((steps,)))

    def at(self, c, where):
        slot = lax.rem(c, self.slots)
        return pltpu.make_async_remote_copy(
            src_ref=self.src(slot, c),
            dst_ref=self.dst(c),
            send_sem=self.send.ref.at[slot],
            recv_sem=self.recv.ref.at[c],
            device_id=where[self.to],
            device_id_type=MESH,
        )


class Ring:
    def __init__(self, pool, axis, steps, rows, cols, staged):
        self.came = [Scratch(pool, pltpu.VMEM((steps, 2, rows, cols), jnp.float32)) for _ in range(2)]
        self.passed = Scratch(pool, pltpu.VMEM((steps, 2, rows, cols), jnp.float32))
        self.copies, self.on = [], []
        if staged:
            self.staged = [Scratch(pool, pltpu.VMEM((SLOTS, 2, rows, cols), jnp.float32)) for _ in range(2)]
        else:
            self.acc = Scratch(pool, pltpu.VMEM((SLOTS, 8, rows, cols), jnp.float32))
        for way in range(2):

            def first(slot, c, way=way):
                return self.staged[way].ref.at[slot] if staged else self.acc.ref.at[slot, pl.ds(2 * way, 2)]

            def landed(c, way=way):
                return self.came[way].ref.at[c]

            def second(slot, c, way=way):
                return self.came[way].ref.at[c, 0]

            def last(c, way=way):
                return self.passed.ref.at[c, way]

            self.copies.append(Copy(pool, axis[way], first, landed, SLOTS, steps))
            self.on.append(Copy(pool, axis[way], second, last, SLOTS, steps))


class Direct:
    def __init__(self, pool, axis, steps, rows, cols, slots=None):
        slots = slots or steps
        self.acc = Scratch(pool, pltpu.VMEM((slots, 4, rows, cols), jnp.float32))
        self.came = Scratch(pool, pltpu.VMEM((steps, 3, rows, cols), jnp.float32))
        self.slots, self.copies = slots, []
        for k, to in ((1, axis[0]), (2, axis[2]), (3, axis[1])):

            def src(slot, c, k=k):
                return self.acc.ref.at[slot, k]

            def dst(c, k=k):
                return self.came.ref.at[c, k - 1]

            self.copies.append(Copy(pool, to, src, dst, slots, steps))


class Fan:
    def __init__(self, pool, steps, rows, cols):
        self.acc = Scratch(pool, pltpu.VMEM((steps, 8, rows, cols), jnp.float32))
        self.came = Scratch(pool, pltpu.VMEM((steps, 8, rows, cols), jnp.float32))
        self.copies = {}
        for at, to in ((1, YH), (2, XP), (3, XPH), (4, X2), (5, X2H), (6, XM), (7, XMH)):

            def src(slot, c, at=at):
                return self.acc.ref.at[c, at]

            def dst(c, at=at):
                return self.came.ref.at[c, at]

            self.copies[at] = Copy(pool, to, src, dst, steps, steps)


class Swap:
    def __init__(self, pool, to, steps, slots, shape):
        self.out = Scratch(pool, pltpu.VMEM((slots, *shape), jnp.float32))
        self.own = Scratch(pool, pltpu.VMEM((slots, *shape), jnp.float32))
        self.came = Scratch(pool, pltpu.VMEM((steps, *shape), jnp.float32))
        self.copy = Copy(
            pool, to, lambda slot, c: self.out.ref.at[slot], lambda c: self.came.ref.at[c], slots, steps
        )


class Side:
    def __init__(self, pool, to, steps, slots, shape):
        self.out = Scratch(pool, pltpu.VMEM((slots, *shape), jnp.float32))
        self.came = Scratch(pool, pltpu.VMEM((steps, *shape), jnp.float32))
        self.copy = Copy(
            pool, to, lambda slot, c: self.out.ref.at[slot], lambda c: self.came.ref.at[c], slots, steps
        )


class Steps:
    def __init__(self, pool, widths, steps, first_column, slots, grad_slots):
        self.widths, self.steps, self.first_column = widths, steps, first_column
        self.cols = sum(widths.values())
        self.start = {X: 0, Z: widths[X], Y: widths[X] + widths[Z]}
        self.slots, self.grad_slots = slots, grad_slots
        self.grad = Scratch(pool, pltpu.VMEM((grad_slots, 512, self.cols), jnp.bfloat16))
        self.grad_sem = Scratch(pool, pltpu.SemaphoreType.DMA((grad_slots,)))
        self.out_sem = Scratch(pool, pltpu.SemaphoreType.DMA((3, slots)))
        self.swap = {t: Swap(pool, YN, steps, slots, (16, widths[t])) for t in (X, Z)}
        self.side = Side(pool, YN, steps, slots, (4, 64, widths[Y]))
        self.core = Swap(pool, CORE, steps, slots, (32, self.cols))

    def columns(self, c, offset=0, width=None):
        return pl.ds(
            pl.multiple_of(self.first_column + c * self.cols + offset, 128), self.cols if width is None else width
        )


def plan():
    pool = []
    state = [Scratch(pool, pltpu.VMEM((16, D), jnp.float32)) for _ in range(3)]
    state_sem = Scratch(pool, pltpu.SemaphoreType.DMA((3,)))
    select = Scratch(pool, pltpu.VMEM((64, 16), jnp.float32))
    wide = Steps(pool, WIDE, WIDE_STEPS, 0, SLOTS, GRAD_SLOTS)
    n = WIDE_STEPS
    wide.level = {
        t: [
            Ring(pool, AXES[t][0], n, 32 if t == Y else 64, WIDE[t], t != Y),
            Ring(pool, AXES[t][1], n, 8 if t == Y else 16, WIDE[t], False),
        ]
        for t in (X, Z, Y)
    }
    wide.yh = Swap(pool, YH, n, SLOTS, (8, WIDE_COLS // 2))
    wide.parity = Direct(pool, AXES[X][0], n, 8, WIDE_COLS, SLOTS)
    wide.fan = Fan(pool, 1, 8, WIDE_COLS // 2)
    n = NARROW_STEPS
    narrow = Steps(pool, NARROW, n, WIDE_STEPS * WIDE_COLS, n, n)
    narrow.level = {
        t: [
            Direct(pool, AXES[t][0], n, 64 if t == Y else 128, NARROW[t]),
            Direct(pool, AXES[t][1], n, 16 if t == Y else 32, NARROW[t]),
        ]
        for t in (X, Z, Y)
    }
    narrow.fan = Fan(pool, n, 8, NARROW_COLS // 2)
    return pool, state, state_sem, select, wide, narrow


def kernel(planned, grads, master, one, two, generator, member_slot, holder, *rest):
    pool, state, state_sem, select, wide, narrow = planned
    outs, parity = rest[:3], rest[3]
    for made, ref in zip(pool, rest[4:], strict=True):
        made.ref = ref
    dp, code = lax.axis_index("dp"), lax.axis_index("code")
    x, yl, z = dp // 8, lax.rem(dp // 4, 2), lax.rem(dp, 4)
    yh, core = code // 2, lax.rem(code, 2)

    def device(x=x, yl=yl, z=z, yh=yh, core=core):
        return (x * 8 + yl * 4 + z, yh * 2 + core)

    def around(at, by):
        return lax.rem(at + by, 4)

    where = {
        XP: device(x=around(x, 1)),
        XM: device(x=around(x, 3)),
        X2: device(x=around(x, 2)),
        ZP: device(z=around(z, 1)),
        ZM: device(z=around(z, 3)),
        Z2: device(z=around(z, 2)),
        YN: device(yl=1 - yl),
        YH: device(yh=1 - yh),
        CORE: device(core=1 - core),
        XPH: device(x=around(x, 1), yh=1 - yh),
        XMH: device(x=around(x, 3), yh=1 - yh),
        X2H: device(x=around(x, 2), yh=1 - yh),
    }
    place = {X: (x, z), Z: (z, x), Y: (z, x)}

    def start(copy, c):
        copy.at(c, where).start()

    def arrive(*copies, c):
        for copy in copies:
            copy.at(c, where).wait_recv()

    def left(*copies, c):
        for copy in copies:
            copy.at(c, where).wait_send()

    def load(s, c):
        slot = lax.rem(c, s.grad_slots)
        return pltpu.make_async_copy(
            grads.at[0, 0, :, s.columns(c)], s.grad.ref.at[slot], s.grad_sem.ref.at[slot]
        )

    given = [
        pltpu.make_async_copy(ref.at[0], held.ref, state_sem.ref.at[at])
        for at, (ref, held) in enumerate(zip((master, one, two), state, strict=True))
    ]

    def store(s, at, c):
        columns = s.columns(c)
        return pltpu.make_async_copy(
            state[at].ref.at[:, columns],
            outs[at].at[0, :, columns],
            s.out_sem.ref.at[at, lax.rem(c, s.slots)],
        )

    def grad(s, t, c, row, rows):
        block = s.grad.ref[
            lax.rem(c, s.grad_slots), pl.ds(pl.multiple_of(row, 16), rows), pl.ds(s.start[t], s.widths[t])
        ]
        return block.astype(jnp.float32)

    def first_row(t, a, h, b):
        return (a * 128 + b * 16 if t == X else a * 16 + b * 128) + h * 64

    def own(s, t, c, a, h):
        if t == X:
            return [(0, 64, grad(s, t, c, first_row(t, a, h, 0), 64))]
        return [(16 * b, 16, grad(s, t, c, first_row(t, a, h, b), 16)) for b in range(4)]

    def fill_side(s, c):
        slot = lax.rem(c, s.slots)
        for b in range(4):
            s.side.out.ref[slot, b] = grad(s, Y, c, b * 128 + (1 - yl) * 64, 64)

    def side_block(s, c, at, b):
        mine = grad(s, Y, c, b * 128 + yl * 64 + at * 16, 16)
        return mine + s.side.came.ref[c, b, pl.ds(pl.multiple_of(at * 16, 16), 16)]

    def adam(s, t, c, summed):
        columns = s.columns(c, s.start[t], s.widths[t])
        held_master, held_one, held_two = (held.ref for held in state)
        weights = held_master[:, columns]
        new_one = beta_one * held_one[:, columns] + (1.0 - beta_one) * summed
        new_two = beta_two * held_two[:, columns] + (1.0 - beta_two) * summed * summed
        direction = new_one / correct_one / (jnp.sqrt(new_two / correct_two) + epsilon)
        held_master[:, columns] = weights - learn_rate * (direction + decay_rate * weights)
        held_one[:, columns] = new_one
        held_two[:, columns] = new_two

    def terms(s, c):
        slot = lax.rem(c, s.slots)
        updated = state[0].ref[:, s.columns(c)]

        def weighted(rows):
            return jnp.dot(
                select.ref[rows], updated, precision=lax.Precision.HIGHEST, preferred_element_type=jnp.float32
            )

        s.core.out.ref[slot] = weighted(pl.ds(32, 32))
        start(s.core.copy, c)
        for at in range(3):
            store(s, at, c).start()
        s.core.own.ref[slot] = weighted(pl.ds(0, 32))

    def end_swaps(s, c, halves):
        slot = lax.rem(c, s.slots)
        for t in (X, Z):
            arrive(s.swap[t].copy, c=c)
            adam(s, t, c, s.swap[t].own.ref[slot] + s.swap[t].came.ref[c])
        adam(s, Y, c, halves)
        terms(s, c)

    def start_swap(s, t, c, low, high):
        slot = lax.rem(c, s.slots)
        s.swap[t].out.ref[slot] = jnp.where(yl == 0, high, low)
        start(s.swap[t].copy, c)
        s.swap[t].own.ref[slot] = jnp.where(yl == 0, low, high)

    def write_parity(s, c, total):
        half = s.cols // 2
        for h in range(2):
            parity[0, :, s.columns(c, half * h, half)] = total[4 * h : 4 * h + 4]

    def both_cores(s, c, k):
        rows = pl.ds(8 * k, 8)
        return s.core.own.ref[lax.rem(c, s.slots), rows] + s.core.came.ref[c, rows]

    def fill_fan(s, c, at):
        fan, half = s.fan, s.cols // 2
        for k in (2, 1, 3, 0):
            block = both_cores(s, c, k)
            for other in (1, 0):
                part = block[4 * other : 4 * other + 4]
                fan.acc.ref[at, 2 * k + other] = jnp.concatenate([part[:, 0:half], part[:, half:]], axis=0)
                if k or other:
                    start(fan.copies[2 * k + other], at)

    def end_fan(s, c, at):
        fan = s.fan
        arrive(*fan.copies.values(), c=at)
        total = fan.acc.ref[at, 0]
        for part in fan.copies:
            total += fan.came.ref[at, part]
        write_parity(s, c, total)
        left(*fan.copies.values(), c=at)


    def pass_on(ring, c, mine):
        for way in range(2):
            arrive(ring.copies[way], c=c)
            for row, rows, value in mine(way):
                ring.came[way].ref[c, 0, pl.ds(row, rows)] += value
            start(ring.on[way], c)

    def held_part(ring, c):
        slot = lax.rem(c, SLOTS)
        rows = ring.acc.spec.shape[2]
        return lambda way: [(0, rows, ring.acc.ref[slot, 4 + way])]

    def grad_part(t, c):
        a = place[t][0]
        return lambda way: own(wide, t, c, around(a, (1, 3)[way]), way)

    def fill_eight(ring, c, block):
        slot = lax.rem(c, SLOTS)

        def put(k, h):
            ring.acc.ref[slot, PLACE[k, h]] = block(k, h)

        put(2, 0)
        put(1, 1)
        start(ring.copies[0], c)
        put(2, 1)
        put(3, 0)
        start(ring.copies[1], c)
        for k, h in ((1, 0), (3, 1), (0, 0), (0, 1)):
            put(k, h)

    def halves(ring, c):
        slot = lax.rem(c, SLOTS)
        arrive(*ring.on, c=c)
        return [
            ring.acc.ref[slot, 6 + h] + ring.came[1 - h].ref[c, 1] + ring.passed.ref[c, h] for h in range(2)
        ]

    def second_axis(t, c):
        slot = lax.rem(c, SLOTS)
        ring, after = wide.level[t]
        r = after.acc.spec.shape[2]
        at_a, at_b = place[t]
        arrive(*ring.on, c=c)

        def block(k, h):
            b = around(at_b, k)
            rows = pl.ds(pl.multiple_of(b * r, r), r)
            if t == Y:
                mine = ring.acc.ref[slot, 6 + h, rows]
            else:
                mine = grad(wide, t, c, first_row(t, at_a, h, b), 16)
            return mine + ring.came[1 - h].ref[c, 1, rows] + ring.passed.ref[c, h, rows]

        fill_eight(after, c, block)

    def fill_wide(c):
        slot = lax.rem(c, SLOTS)
        load(wide, c).wait()
        fill_side(wide, c)
        for t in (X, Z):
            ring, a = wide.level[t][0], place[t][0]
            for way, parts in enumerate((((2, 0), (1, 1)), ((2, 1), (3, 0)))):
                for at, (k, h) in enumerate(parts):
                    for row, rows, value in own(wide, t, c, around(a, k), h):
                        ring.staged[way].ref[slot, at, pl.ds(row, rows)] = value

    def wide0(c):
        start(wide.side.copy, c)
        for way in range(2):
            for t in (X, Z):
                start(wide.level[t][0].copies[way], c)

    def wide1(c):
        slot = lax.rem(c, SLOTS)
        for t in (X, Z):
            pass_on(wide.level[t][0], c, grad_part(t, c))
        arrive(wide.side.copy, c=c)
        ring = wide.level[Y][0]

        def block(k):
            at = around(z, k)
            for b in range(4):
                total = side_block(wide, c, at, b)
                for h in range(2):
                    ring.acc.ref[slot, PLACE[k, h], pl.ds(8 * b, 8)] = total[8 * h : 8 * h + 8]

        block(2)
        block(1)
        start(ring.copies[0], c)
        block(3)
        start(ring.copies[1], c)
        block(0)

    def wide2(c):
        left(*wide.level[X][0].copies, *wide.level[Z][0].copies, wide.side.copy, c=c)
        for t in (X, Z):
            second_axis(t, c)
        pass_on(wide.level[Y][0], c, held_part(wide.level[Y][0], c))

    def wide3(c):
        left(*wide.level[X][0].on, *wide.level[Z][0].on, *wide.level[Y][0].copies, c=c)
        for t in (X, Z):
            pass_on(wide.level[t][1], c, held_part(wide.level[t][1], c))
        second_axis(Y, c)

    def wide4(c):
        left(*wide.level[X][1].copies, *wide.level[Z][1].copies, *wide.level[Y][0].on, c=c)
        for t in (X, Z):
            start_swap(wide, t, c, *halves(wide.level[t][1], c))
        pass_on(wide.level[Y][1], c, held_part(wide.level[Y][1], c))

    def wide5(c):
        left(*wide.level[X][1].on, *wide.level[Z][1].on, *wide.level[Y][1].copies, c=c)

        @pl.when(c == 0)
        def _():
            for copy in given:
                copy.wait()

        end_swaps(wide, c, jnp.concatenate(halves(wide.level[Y][1], c), axis=0))

    def wide6(c):
        arrive(wide.core.copy, c=c)

        @pl.when(c < WIDE_STEPS - 1)
        def _():
            slot = lax.rem(c, SLOTS)

            def block(k):
                wide.parity.acc.ref[slot, k] = both_cores(wide, c, k)

            fill_four(wide.parity, c, block)

        @pl.when(c == WIDE_STEPS - 1)
        def _():
            fill_fan(wide, c, 0)

    def settle(c):
        left(wide.swap[X].copy, wide.swap[Z].copy, *wide.level[Y][1].on, wide.core.copy, c=c)
        for at in range(3):
            store(wide, at, c).wait()

    def wide7(c):
        slot, half = lax.rem(c, SLOTS), WIDE_COLS // 2
        total = whole(wide.parity, c)
        low, high = total[:, 0:half], total[:, half:]
        wide.yh.out.ref[slot] = jnp.concatenate([low[4:8], high[4:8]], axis=0)
        start(wide.yh.copy, c)
        wide.yh.own.ref[slot] = jnp.concatenate([low[0:4], high[0:4]], axis=0)
        settle(c)

    def wide8(c):
        left(*wide.parity.copies, c=c)
        arrive(wide.yh.copy, c=c)
        write_parity(wide, c, wide.yh.own.ref[lax.rem(c, SLOTS)] + wide.yh.came.ref[c])
        left(wide.yh.copy, c=c)

    def wide_end(_):
        end_fan(wide, WIDE_STEPS - 1, 0)
        settle(WIDE_STEPS - 1)


    def fill_four(level, c, block):
        for k in (2, 1, 3):
            block(k)
            start(level.copies[k - 1], c)
        block(0)

    def whole(level, c):
        arrive(*level.copies, c=c)
        acc, came = level.acc.ref, level.came.ref
        return (acc[lax.rem(c, level.slots), 0] + came[c, 0]) + (came[c, 1] + came[c, 2])

    def fill_narrow(c):
        load(narrow, c).wait()
        fill_side(narrow, c)
        for t in (X, Z):
            for k in range(4):
                for h in range(2):
                    for row, rows, value in own(narrow, t, c, around(place[t][0], k), h):
                        narrow.level[t][0].acc.ref[c, k, pl.ds(64 * h + row, rows)] = value

    def narrow0(c):
        start(narrow.side.copy, c)
        for k in (2, 1, 3):
            for t in (X, Z):
                start(narrow.level[t][0].copies[k - 1], c)

    def narrow1(c):
        for t in (X, Z):
            level, after = narrow.level[t]
            arrive(*level.copies, c=c)

            def block(k, t=t, level=level, after=after):
                b = around(place[t][1], k)
                for h in range(2):
                    rows = pl.ds(pl.multiple_of(64 * h + 16 * b, 16), 16)
                    acc, came = level.acc.ref, level.came.ref
                    after.acc.ref[c, k, pl.ds(16 * h, 16)] = (acc[c, 0, rows] + came[c, 0, rows]) + (
                        came[c, 1, rows] + came[c, 2, rows]
                    )

            fill_four(after, c, block)
        arrive(narrow.side.copy, c=c)
        level = narrow.level[Y][0]

        def side(k):
            for b in range(4):
                level.acc.ref[c, k, pl.ds(16 * b, 16)] = side_block(narrow, c, around(z, k), b)

        fill_four(level, c, side)

    def narrow2(c):
        for t in (X, Z):
            both = whole(narrow.level[t][1], c)
            start_swap(narrow, t, c, both[0:16], both[16:32])
        level, after = narrow.level[Y]
        arrive(*level.copies, c=c)

        def block(k):
            rows = pl.ds(pl.multiple_of(16 * around(x, k), 16), 16)
            acc, came = level.acc.ref, level.came.ref
            after.acc.ref[c, k] = (acc[c, 0, rows] + came[c, 0, rows]) + (came[c, 1, rows] + came[c, 2, rows])

        fill_four(after, c, block)

    def narrow3(c):
        end_swaps(narrow, c, whole(narrow.level[Y][1], c))

    def narrow4(c):
        arrive(narrow.core.copy, c=c)
        fill_fan(narrow, c, c)

    def narrow5(c):
        end_fan(narrow, c, c)
        for t in (X, Z):
            left(*narrow.level[t][0].copies, *narrow.level[t][1].copies, narrow.swap[t].copy, c=c)
        left(*narrow.level[Y][0].copies, *narrow.level[Y][1].copies, narrow.side.copy, c=c)
        left(narrow.core.copy, c=c)
        for at in range(3):
            store(narrow, at, c).wait()

    def selector():
        def iota(shape, dimension):
            return lax.broadcasted_iota(jnp.int32, shape, dimension)

        def parts(shape):
            row = iota(shape, 0)
            d = row // 4
            first = lax.rem(x + lax.rem(d // 2, 4), 4) * 8 + lax.rem(dp, 8)
            second = lax.rem(yh + lax.rem(d, 2), 2) * 2 + lax.rem(core + d // 8, 2)
            return first, second, lax.rem(row, 4).astype(jnp.float32)

        first, second, _ = parts((64, 32))
        held = holder[...].astype(jnp.float32)
        mask = first == iota((64, 32), 1)
        picked = jnp.zeros((64, 32), jnp.float32)
        for at in range(4):
            picked += jnp.where(mask & (second == at), held[at : at + 1, :], 0.0)
        block = jnp.sum(picked, axis=1, keepdims=True)
        lane = iota((64, 16), 1)
        lane_value = lane.astype(jnp.float32)
        hit = lane_value == block
        column = jnp.sum(
            jnp.where(iota((4, 16), 1) == member_slot[...], generator[...], 0.0), axis=1, keepdims=True
        )
        spread = jnp.sum(jnp.where(iota((4, 16), 0) == iota((4, 16), 1) // 4, column, 0.0), axis=0, keepdims=True)
        scale = jnp.sum(jnp.where(hit, spread, 0.0), axis=1, keepdims=True)
        quarter = jnp.sum(
            jnp.where(hit, lax.rem(lane, 4).astype(jnp.float32), 0.0), axis=1, keepdims=True
        )
        _, _, row_in = parts((64, 16))
        select.ref[...] = jnp.where(lane_value == quarter * 4.0 + row_in, scale, 0.0)

    def load_rest():
        for c in range(2, GRAD_SLOTS - 1):
            load(wide, c).start()
        for copy in given:
            copy.start()
        for c in range(NARROW_STEPS):
            load(narrow, c).start()
        selector()

    load(wide, 0).start()
    barrier = pltpu.get_barrier_semaphore()
    for to in where.values():
        pl.semaphore_signal(barrier, inc=1, device_id=to, device_id_type=MESH)
    fill_wide(0)
    load(wide, 1).start()
    pl.semaphore_wait(barrier, len(where))

    first, wide_last, last = WIDE_STEPS, WIDE_STEPS - 1, NARROW_STEPS - 1
    turn = (
        (wide0, 0, wide_last), (narrow0, first, first + last),
        (wide1, 1, wide_last + 1), (narrow1, first + 1, first + 1 + last),
        (wide2, 2, wide_last + 2), (narrow2, first + 2, first + 2 + last),
        (wide3, 3, wide_last + 3), (narrow3, first + 3, first + 3 + last),
        (wide4, 4, wide_last + 4), (wide5, 5, wide_last + 5),
        (narrow4, first + 3, first + 3 + last), (wide7, 6, wide_last + 5),
        (narrow5, first + 4, first + 4 + last), (wide8, 7, wide_last + 6),
        (wide_end, wide_last + 6, wide_last + 6),
        (fill_wide, -1, wide_last - 1), (fill_narrow, first - 1, first - 1 + last),
        (wide6, 5, wide_last + 5),
    )
    turns = 1 + max(end for _, _, end in turn)

    def step(t, carry):
        for stage, begin, end in turn:

            @pl.when((t >= begin) & (t <= end))
            def _(stage=stage, begin=begin):
                stage(t - begin)

        @pl.when(t == 0)
        def _():
            load_rest()

        @pl.when((t > 0) & (t + GRAD_SLOTS - 2 < WIDE_STEPS))
        def _():
            load(wide, t + GRAD_SLOTS - 2).start()

        return carry

    lax.fori_loop(0, turns, step, 0)


def finish(count, *refs):
    given, outs, held = refs[:count], refs[count : 2 * count], refs[2 * count : 3 * count]
    sem = refs[3 * count]
    parts = []
    for at in range(count):
        pieces = 4 if given[at].shape[1] % 16 == 0 else 1
        columns = given[at].shape[2] // pieces
        for piece in range(pieces):
            part = (slice(None), slice(None), pl.ds(piece * columns, columns))
            parts.append(
                (
                    pltpu.make_async_copy(given[at].at[part], held[at].at[part], sem.at[0, at, piece]),
                    pltpu.make_async_copy(held[at].at[part], outs[at].at[part], sem.at[1, at, piece]),
                )
            )
    for read, _ in parts:
        read.start()
    for read, write in parts:
        read.wait()
        write.start()
    for _, write in parts:
        write.wait()


def shards(grads, master, moment_one, moment_two, generator, member_slot, holder):
    planned = plan()
    anywhere = pl.BlockSpec(memory_space=pl.ANY)
    vmem = pl.BlockSpec(memory_space=pltpu.VMEM)
    state = jax.ShapeDtypeStruct(master.shape, jnp.float32)
    made = (state, state, state, jax.ShapeDtypeStruct((1, 4, D), jnp.float32))
    results = pl.pallas_call(
        functools.partial(kernel, planned),
        out_shape=made,
        in_specs=[anywhere] * 4 + [vmem] * 3,
        out_specs=(anywhere, anywhere, anywhere, vmem),
        scratch_shapes=[part.spec for part in planned[0]],
        name="adam_parity",
        compiler_params=pltpu.CompilerParams(
            collective_id=0, has_side_effects=True, vmem_limit_bytes=63 * 2**20
        ),
    )(grads, master, moment_one, moment_two, generator, member_slot, holder.T)
    return pl.pallas_call(
        functools.partial(finish, 4),
        out_shape=made,
        in_specs=[anywhere] * 4,
        out_specs=(anywhere,) * 4,
        scratch_shapes=[pltpu.VMEM(part.shape, part.dtype) for part in made] + [pltpu.SemaphoreType.DMA((2, 4, 4))],
        name="write_out",
        compiler_params=pltpu.CompilerParams(vmem_limit_bytes=63 * 2**20),
    )(*results)


def solution(mesh):
    state = P("code", "dp", None)
    return jax.shard_map(
        shards,
        mesh=mesh,
        in_specs=(P("dp", "code", None, None), state, state, state, P(), P("dp", "code"), P()),
        out_specs=(state, state, state, state),
        check_vma=False,
    )
```

```python
import functools

import jax
import jax.numpy as jnp
from jax import lax
from jax.experimental import pallas as pl
from jax.experimental.pallas import tpu as pltpu
from jax.sharding import PartitionSpec as P

MESH = pl.DeviceIdType.MESH

beta_one = 0.9
beta_two = 0.999
learn_rate = 0.05
decay_rate = 0.1
epsilon = 1e-08
correct_one = 1.0 - 0.9**10
correct_two = 1.0 - 0.999**10

D = 16384
X, Z, Y = range(3)
XP, XM, X2, ZP, ZM, Z2, YN, YH, CORE, XPH, XMH, X2H = range(12)
AXES = {X: ((XP, XM, X2), (ZP, ZM, Z2)), Z: ((ZP, ZM, Z2), (XP, XM, X2)), Y: ((ZP, ZM, Z2), (XP, XM, X2))}
WIDE = {X: 384, Z: 256, Y: 384}
WIDE_STEPS = 15
NARROW = {X: 128, Z: 128, Y: 256}
NARROW_STEPS = 2
WIDE_COLS, NARROW_COLS = sum(WIDE.values()), sum(NARROW.values())
GRAD_SLOTS = 5
SLOTS = 3
PLACE = {(2, 0): 0, (1, 1): 1, (2, 1): 2, (3, 0): 3, (1, 0): 4, (3, 1): 5, (0, 0): 6, (0, 1): 7}

assert WIDE_COLS * WIDE_STEPS + NARROW_COLS * NARROW_STEPS == D


class Scratch:
    def __init__(self, pool, spec):
        self.spec, self.ref = spec, None
        pool.append(self)


class Copy:
    def __init__(self, pool, to, src, dst, slots, steps):
        self.to, self.src, self.dst, self.slots = to, src, dst, slots
        self.send = Scratch(pool, pltpu.SemaphoreType.DMA((slots,)))
        self.recv = Scratch(pool, pltpu.SemaphoreType.DMA((steps,)))

    def at(self, c, where):
        slot = lax.rem(c, self.slots)
        return pltpu.make_async_remote_copy(
            src_ref=self.src(slot, c),
            dst_ref=self.dst(c),
            send_sem=self.send.ref.at[slot],
            recv_sem=self.recv.ref.at[c],
            device_id=where[self.to],
            device_id_type=MESH,
        )


class Ring:
    def __init__(self, pool, axis, steps, rows, cols, staged):
        self.came = [Scratch(pool, pltpu.VMEM((steps, 2, rows, cols), jnp.float32)) for _ in range(2)]
        self.passed = Scratch(pool, pltpu.VMEM((steps, 2, rows, cols), jnp.float32))
        self.copies, self.on = [], []
        if staged:
            self.staged = [Scratch(pool, pltpu.VMEM((SLOTS, 2, rows, cols), jnp.float32)) for _ in range(2)]
        else:
            self.acc = Scratch(pool, pltpu.VMEM((SLOTS, 8, rows, cols), jnp.float32))
        for way in range(2):

            def first(slot, c, way=way):
                return self.staged[way].ref.at[slot] if staged else self.acc.ref.at[slot, pl.ds(2 * way, 2)]

            def landed(c, way=way):
                return self.came[way].ref.at[c]

            def second(slot, c, way=way):
                return self.came[way].ref.at[c, 0]

            def last(c, way=way):
                return self.passed.ref.at[c, way]

            self.copies.append(Copy(pool, axis[way], first, landed, SLOTS, steps))
            self.on.append(Copy(pool, axis[way], second, last, SLOTS, steps))


class Direct:
    def __init__(self, pool, axis, steps, rows, cols, slots=None):
        slots = slots or steps
        self.acc = Scratch(pool, pltpu.VMEM((slots, 4, rows, cols), jnp.float32))
        self.came = Scratch(pool, pltpu.VMEM((steps, 3, rows, cols), jnp.float32))
        self.slots, self.copies = slots, []
        for k, to in ((1, axis[0]), (2, axis[2]), (3, axis[1])):

            def src(slot, c, k=k):
                return self.acc.ref.at[slot, k]

            def dst(c, k=k):
                return self.came.ref.at[c, k - 1]

            self.copies.append(Copy(pool, to, src, dst, slots, steps))


class Fan:
    def __init__(self, pool, steps, rows, cols):
        self.acc = Scratch(pool, pltpu.VMEM((steps, 8, rows, cols), jnp.float32))
        self.came = Scratch(pool, pltpu.VMEM((steps, 8, rows, cols), jnp.float32))
        self.copies = {}
        for at, to in ((1, YH), (2, XP), (3, XPH), (4, X2), (5, X2H), (6, XM), (7, XMH)):

            def src(slot, c, at=at):
                return self.acc.ref.at[c, at]

            def dst(c, at=at):
                return self.came.ref.at[c, at]

            self.copies[at] = Copy(pool, to, src, dst, steps, steps)


class Swap:
    def __init__(self, pool, to, steps, slots, shape):
        self.out = Scratch(pool, pltpu.VMEM((slots, *shape), jnp.float32))
        self.own = Scratch(pool, pltpu.VMEM((slots, *shape), jnp.float32))
        self.came = Scratch(pool, pltpu.VMEM((steps, *shape), jnp.float32))
        self.copy = Copy(
            pool, to, lambda slot, c: self.out.ref.at[slot], lambda c: self.came.ref.at[c], slots, steps
        )


class Side:
    def __init__(self, pool, to, steps, slots, shape):
        self.out = Scratch(pool, pltpu.VMEM((slots, *shape), jnp.float32))
        self.came = Scratch(pool, pltpu.VMEM((steps, *shape), jnp.float32))
        self.copy = Copy(
            pool, to, lambda slot, c: self.out.ref.at[slot], lambda c: self.came.ref.at[c], slots, steps
        )


class Steps:
    def __init__(self, pool, widths, steps, first_column, slots, grad_slots):
        self.widths, self.steps, self.first_column = widths, steps, first_column
        self.cols = sum(widths.values())
        self.start = {X: 0, Z: widths[X], Y: widths[X] + widths[Z]}
        self.slots, self.grad_slots = slots, grad_slots
        self.grad = Scratch(pool, pltpu.VMEM((grad_slots, 512, self.cols), jnp.bfloat16))
        self.grad_sem = Scratch(pool, pltpu.SemaphoreType.DMA((grad_slots,)))
        self.out_sem = Scratch(pool, pltpu.SemaphoreType.DMA((3, slots)))
        self.swap = {t: Swap(pool, YN, steps, slots, (16, widths[t])) for t in (X, Z)}
        self.side = Side(pool, YN, steps, slots, (4, 64, widths[Y]))
        self.core = Swap(pool, CORE, steps, slots, (32, self.cols))

    def columns(self, c, offset=0, width=None):
        return pl.ds(
            pl.multiple_of(self.first_column + c * self.cols + offset, 128), self.cols if width is None else width
        )


def plan():
    pool = []
    state = [Scratch(pool, pltpu.VMEM((16, D), jnp.float32)) for _ in range(3)]
    state_sem = Scratch(pool, pltpu.SemaphoreType.DMA((3,)))
    select = Scratch(pool, pltpu.VMEM((64, 16), jnp.float32))
    wide = Steps(pool, WIDE, WIDE_STEPS, 0, SLOTS, GRAD_SLOTS)
    n = WIDE_STEPS
    wide.level = {
        t: [
            Ring(pool, AXES[t][0], n, 32 if t == Y else 64, WIDE[t], t != Y),
            Ring(pool, AXES[t][1], n, 8 if t == Y else 16, WIDE[t], False),
        ]
        for t in (X, Z, Y)
    }
    wide.yh = Swap(pool, YH, n, SLOTS, (8, WIDE_COLS // 2))
    wide.parity = Direct(pool, AXES[X][0], n, 8, WIDE_COLS, SLOTS)
    wide.fan = Fan(pool, 1, 8, WIDE_COLS // 2)
    n = NARROW_STEPS
    narrow = Steps(pool, NARROW, n, WIDE_STEPS * WIDE_COLS, n, n)
    narrow.level = {
        t: [
            Direct(pool, AXES[t][0], n, 64 if t == Y else 128, NARROW[t]),
            Direct(pool, AXES[t][1], n, 16 if t == Y else 32, NARROW[t]),
        ]
        for t in (X, Z, Y)
    }
    narrow.fan = Fan(pool, n, 8, NARROW_COLS // 2)
    return pool, state, state_sem, select, wide, narrow


def kernel(planned, grads, master, one, two, generator, member_slot, holder, *rest):
    pool, state, state_sem, select, wide, narrow = planned
    outs, parity = rest[:3], rest[3]
    for made, ref in zip(pool, rest[4:], strict=True):
        made.ref = ref
    dp, code = lax.axis_index("dp"), lax.axis_index("code")
    x, yl, z = dp // 8, lax.rem(dp // 4, 2), lax.rem(dp, 4)
    yh, core = code // 2, lax.rem(code, 2)

    def device(x=x, yl=yl, z=z, yh=yh, core=core):
        return (x * 8 + yl * 4 + z, yh * 2 + core)

    def around(at, by):
        return lax.rem(at + by, 4)

    where = {
        XP: device(x=around(x, 1)),
        XM: device(x=around(x, 3)),
        X2: device(x=around(x, 2)),
        ZP: device(z=around(z, 1)),
        ZM: device(z=around(z, 3)),
        Z2: device(z=around(z, 2)),
        YN: device(yl=1 - yl),
        YH: device(yh=1 - yh),
        CORE: device(core=1 - core),
        XPH: device(x=around(x, 1), yh=1 - yh),
        XMH: device(x=around(x, 3), yh=1 - yh),
        X2H: device(x=around(x, 2), yh=1 - yh),
    }
    place = {X: (x, z), Z: (z, x), Y: (z, x)}

    def start(copy, c):
        copy.at(c, where).start()

    def arrive(*copies, c):
        for copy in copies:
            copy.at(c, where).wait_recv()

    def left(*copies, c):
        for copy in copies:
            copy.at(c, where).wait_send()

    def load(s, c):
        slot = lax.rem(c, s.grad_slots)
        return pltpu.make_async_copy(
            grads.at[0, 0, :, s.columns(c)], s.grad.ref.at[slot], s.grad_sem.ref.at[slot]
        )

    given = [
        pltpu.make_async_copy(ref.at[0], held.ref, state_sem.ref.at[at])
        for at, (ref, held) in enumerate(zip((master, one, two), state, strict=True))
    ]

    def store(s, at, c):
        columns = s.columns(c)
        return pltpu.make_async_copy(
            state[at].ref.at[:, columns],
            outs[at].at[0, :, columns],
            s.out_sem.ref.at[at, lax.rem(c, s.slots)],
        )

    def grad(s, t, c, row, rows):
        block = s.grad.ref[
            lax.rem(c, s.grad_slots), pl.ds(pl.multiple_of(row, 16), rows), pl.ds(s.start[t], s.widths[t])
        ]
        return block.astype(jnp.float32)

    def first_row(t, a, h, b):
        return (a * 128 + b * 16 if t == X else a * 16 + b * 128) + h * 64

    def own(s, t, c, a, h):
        if t == X:
            return [(0, 64, grad(s, t, c, first_row(t, a, h, 0), 64))]
        return [(16 * b, 16, grad(s, t, c, first_row(t, a, h, b), 16)) for b in range(4)]

    def fill_side(s, c):
        slot = lax.rem(c, s.slots)
        for b in range(4):
            s.side.out.ref[slot, b] = grad(s, Y, c, b * 128 + (1 - yl) * 64, 64)

    def side_block(s, c, at, b):
        mine = grad(s, Y, c, b * 128 + yl * 64 + at * 16, 16)
        return mine + s.side.came.ref[c, b, pl.ds(pl.multiple_of(at * 16, 16), 16)]

    def adam(s, t, c, summed):
        columns = s.columns(c, s.start[t], s.widths[t])
        held_master, held_one, held_two = (held.ref for held in state)
        weights = held_master[:, columns]
        new_one = beta_one * held_one[:, columns] + (1.0 - beta_one) * summed
        new_two = beta_two * held_two[:, columns] + (1.0 - beta_two) * summed * summed
        direction = new_one / correct_one / (jnp.sqrt(new_two / correct_two) + epsilon)
        held_master[:, columns] = weights - learn_rate * (direction + decay_rate * weights)
        held_one[:, columns] = new_one
        held_two[:, columns] = new_two

    def terms(s, c):
        slot = lax.rem(c, s.slots)
        updated = state[0].ref[:, s.columns(c)]

        def weighted(rows):
            return jnp.dot(
                select.ref[rows], updated, precision=lax.Precision.HIGHEST, preferred_element_type=jnp.float32
            )

        s.core.out.ref[slot] = weighted(pl.ds(32, 32))
        start(s.core.copy, c)
        for at in range(3):
            store(s, at, c).start()
        s.core.own.ref[slot] = weighted(pl.ds(0, 32))

    def end_swaps(s, c, halves):
        slot = lax.rem(c, s.slots)
        for t in (X, Z):
            arrive(s.swap[t].copy, c=c)
            adam(s, t, c, s.swap[t].own.ref[slot] + s.swap[t].came.ref[c])
        adam(s, Y, c, halves)
        terms(s, c)

    def start_swap(s, t, c, low, high):
        slot = lax.rem(c, s.slots)
        s.swap[t].out.ref[slot] = jnp.where(yl == 0, high, low)
        start(s.swap[t].copy, c)
        s.swap[t].own.ref[slot] = jnp.where(yl == 0, low, high)

    def write_parity(s, c, total):
        half = s.cols // 2
        for h in range(2):
            parity[0, :, s.columns(c, half * h, half)] = total[4 * h : 4 * h + 4]

    def both_cores(s, c, k):
        rows = pl.ds(8 * k, 8)
        return s.core.own.ref[lax.rem(c, s.slots), rows] + s.core.came.ref[c, rows]

    def fill_fan(s, c, at):
        fan, half = s.fan, s.cols // 2
        for k in (2, 1, 3, 0):
            block = both_cores(s, c, k)
            for other in (1, 0):
                part = block[4 * other : 4 * other + 4]
                fan.acc.ref[at, 2 * k + other] = jnp.concatenate([part[:, 0:half], part[:, half:]], axis=0)
                if k or other:
                    start(fan.copies[2 * k + other], at)

    def end_fan(s, c, at):
        fan = s.fan
        arrive(*fan.copies.values(), c=at)
        total = fan.acc.ref[at, 0]
        for part in fan.copies:
            total += fan.came.ref[at, part]
        write_parity(s, c, total)
        left(*fan.copies.values(), c=at)


    def pass_on(ring, c, mine):
        for way in range(2):
            arrive(ring.copies[way], c=c)
            for row, rows, value in mine(way):
                ring.came[way].ref[c, 0, pl.ds(row, rows)] += value
            start(ring.on[way], c)

    def held_part(ring, c):
        slot = lax.rem(c, SLOTS)
        rows = ring.acc.spec.shape[2]
        return lambda way: [(0, rows, ring.acc.ref[slot, 4 + way])]

    def grad_part(t, c):
        a = place[t][0]
        return lambda way: own(wide, t, c, around(a, (1, 3)[way]), way)

    def fill_eight(ring, c, block):
        slot = lax.rem(c, SLOTS)

        def put(k, h):
            ring.acc.ref[slot, PLACE[k, h]] = block(k, h)

        put(2, 0)
        put(1, 1)
        start(ring.copies[0], c)
        put(2, 1)
        put(3, 0)
        start(ring.copies[1], c)
        for k, h in ((1, 0), (3, 1), (0, 0), (0, 1)):
            put(k, h)

    def halves(ring, c):
        slot = lax.rem(c, SLOTS)
        arrive(*ring.on, c=c)
        return [
            ring.acc.ref[slot, 6 + h] + ring.came[1 - h].ref[c, 1] + ring.passed.ref[c, h] for h in range(2)
        ]

    def second_axis(t, c):
        slot = lax.rem(c, SLOTS)
        ring, after = wide.level[t]
        r = after.acc.spec.shape[2]
        at_a, at_b = place[t]
        arrive(*ring.on, c=c)

        def block(k, h):
            b = around(at_b, k)
            rows = pl.ds(pl.multiple_of(b * r, r), r)
            if t == Y:
                mine = ring.acc.ref[slot, 6 + h, rows]
            else:
                mine = grad(wide, t, c, first_row(t, at_a, h, b), 16)
            return mine + ring.came[1 - h].ref[c, 1, rows] + ring.passed.ref[c, h, rows]

        fill_eight(after, c, block)

    def fill_wide(c):
        slot = lax.rem(c, SLOTS)
        load(wide, c).wait()
        fill_side(wide, c)
        for t in (X, Z):
            ring, a = wide.level[t][0], place[t][0]
            for way, parts in enumerate((((2, 0), (1, 1)), ((2, 1), (3, 0)))):
                for at, (k, h) in enumerate(parts):
                    for row, rows, value in own(wide, t, c, around(a, k), h):
                        ring.staged[way].ref[slot, at, pl.ds(row, rows)] = value

    def wide0(c):
        start(wide.side.copy, c)
        for way in range(2):
            for t in (X, Z):
                start(wide.level[t][0].copies[way], c)

    def wide1(c):
        for t in (X, Z):
            pass_on(wide.level[t][0], c, grad_part(t, c))

    def wide1_side(c):
        slot = lax.rem(c, SLOTS)
        arrive(wide.side.copy, c=c)
        ring = wide.level[Y][0]

        def block(k):
            at = around(z, k)
            for b in range(4):
                total = side_block(wide, c, at, b)
                for h in range(2):
                    ring.acc.ref[slot, PLACE[k, h], pl.ds(8 * b, 8)] = total[8 * h : 8 * h + 8]

        block(2)
        block(1)
        start(ring.copies[0], c)
        block(3)
        start(ring.copies[1], c)
        block(0)

    def wide2(c):
        for t in (X, Z):
            second_axis(t, c)

    def wide2_side(c):
        left(*wide.level[X][0].copies, *wide.level[Z][0].copies, wide.side.copy, c=c)
        pass_on(wide.level[Y][0], c, held_part(wide.level[Y][0], c))

    def wide3(c):
        for t in (X, Z):
            pass_on(wide.level[t][1], c, held_part(wide.level[t][1], c))

    def wide3_side(c):
        left(*wide.level[X][0].on, *wide.level[Z][0].on, *wide.level[Y][0].copies, c=c)
        second_axis(Y, c)

    def wide4(c):
        for t in (X, Z):
            start_swap(wide, t, c, *halves(wide.level[t][1], c))

    def wide4_side(c):
        left(*wide.level[X][1].copies, *wide.level[Z][1].copies, *wide.level[Y][0].on, c=c)
        pass_on(wide.level[Y][1], c, held_part(wide.level[Y][1], c))

    def wide5(c):
        left(*wide.level[X][1].on, *wide.level[Z][1].on, *wide.level[Y][1].copies, c=c)

        @pl.when(c == 0)
        def _():
            for copy in given:
                copy.wait()

        end_swaps(wide, c, jnp.concatenate(halves(wide.level[Y][1], c), axis=0))

    def wide6(c):
        arrive(wide.core.copy, c=c)

        @pl.when(c < WIDE_STEPS - 1)
        def _():
            slot = lax.rem(c, SLOTS)

            def block(k):
                wide.parity.acc.ref[slot, k] = both_cores(wide, c, k)

            fill_four(wide.parity, c, block)

        @pl.when(c == WIDE_STEPS - 1)
        def _():
            fill_fan(wide, c, 0)

    def settle(c):
        left(wide.swap[X].copy, wide.swap[Z].copy, *wide.level[Y][1].on, wide.core.copy, c=c)
        for at in range(3):
            store(wide, at, c).wait()

    def wide7(c):
        slot, half = lax.rem(c, SLOTS), WIDE_COLS // 2
        total = whole(wide.parity, c)
        low, high = total[:, 0:half], total[:, half:]
        wide.yh.out.ref[slot] = jnp.concatenate([low[4:8], high[4:8]], axis=0)
        start(wide.yh.copy, c)
        wide.yh.own.ref[slot] = jnp.concatenate([low[0:4], high[0:4]], axis=0)
        settle(c)

    def wide8(c):
        left(*wide.parity.copies, c=c)
        arrive(wide.yh.copy, c=c)
        write_parity(wide, c, wide.yh.own.ref[lax.rem(c, SLOTS)] + wide.yh.came.ref[c])
        left(wide.yh.copy, c=c)

    def wide_end(_):
        end_fan(wide, WIDE_STEPS - 1, 0)
        settle(WIDE_STEPS - 1)


    def fill_four(level, c, block):
        for k in (2, 1, 3):
            block(k)
            start(level.copies[k - 1], c)
        block(0)

    def whole(level, c):
        arrive(*level.copies, c=c)
        acc, came = level.acc.ref, level.came.ref
        return (acc[lax.rem(c, level.slots), 0] + came[c, 0]) + (came[c, 1] + came[c, 2])

    def fill_narrow(c):
        load(narrow, c).wait()
        fill_side(narrow, c)
        for t in (X, Z):
            for k in range(4):
                for h in range(2):
                    for row, rows, value in own(narrow, t, c, around(place[t][0], k), h):
                        narrow.level[t][0].acc.ref[c, k, pl.ds(64 * h + row, rows)] = value

    def narrow0(c):
        start(narrow.side.copy, c)
        for k in (2, 1, 3):
            for t in (X, Z):
                start(narrow.level[t][0].copies[k - 1], c)

    def narrow1(c):
        for t in (X, Z):
            level, after = narrow.level[t]
            arrive(*level.copies, c=c)

            def block(k, t=t, level=level, after=after):
                b = around(place[t][1], k)
                for h in range(2):
                    rows = pl.ds(pl.multiple_of(64 * h + 16 * b, 16), 16)
                    acc, came = level.acc.ref, level.came.ref
                    after.acc.ref[c, k, pl.ds(16 * h, 16)] = (acc[c, 0, rows] + came[c, 0, rows]) + (
                        came[c, 1, rows] + came[c, 2, rows]
                    )

            fill_four(after, c, block)
        arrive(narrow.side.copy, c=c)
        level = narrow.level[Y][0]

        def side(k):
            for b in range(4):
                level.acc.ref[c, k, pl.ds(16 * b, 16)] = side_block(narrow, c, around(z, k), b)

        fill_four(level, c, side)

    def narrow2(c):
        for t in (X, Z):
            both = whole(narrow.level[t][1], c)
            start_swap(narrow, t, c, both[0:16], both[16:32])
        level, after = narrow.level[Y]
        arrive(*level.copies, c=c)

        def block(k):
            rows = pl.ds(pl.multiple_of(16 * around(x, k), 16), 16)
            acc, came = level.acc.ref, level.came.ref
            after.acc.ref[c, k] = (acc[c, 0, rows] + came[c, 0, rows]) + (came[c, 1, rows] + came[c, 2, rows])

        fill_four(after, c, block)

    def narrow3(c):
        end_swaps(narrow, c, whole(narrow.level[Y][1], c))

    def narrow4(c):
        arrive(narrow.core.copy, c=c)
        fill_fan(narrow, c, c)

    def narrow5(c):
        end_fan(narrow, c, c)
        for t in (X, Z):
            left(*narrow.level[t][0].copies, *narrow.level[t][1].copies, narrow.swap[t].copy, c=c)
        left(*narrow.level[Y][0].copies, *narrow.level[Y][1].copies, narrow.side.copy, c=c)
        left(narrow.core.copy, c=c)
        for at in range(3):
            store(narrow, at, c).wait()

    def selector():
        def iota(shape, dimension):
            return lax.broadcasted_iota(jnp.int32, shape, dimension)

        def parts(shape):
            row = iota(shape, 0)
            d = row // 4
            first = lax.rem(x + lax.rem(d // 2, 4), 4) * 8 + lax.rem(dp, 8)
            second = lax.rem(yh + lax.rem(d, 2), 2) * 2 + lax.rem(core + d // 8, 2)
            return first, second, lax.rem(row, 4).astype(jnp.float32)

        first, second, _ = parts((64, 32))
        held = holder[...].astype(jnp.float32)
        mask = first == iota((64, 32), 1)
        picked = jnp.zeros((64, 32), jnp.float32)
        for at in range(4):
            picked += jnp.where(mask & (second == at), held[at : at + 1, :], 0.0)
        block = jnp.sum(picked, axis=1, keepdims=True)
        lane = iota((64, 16), 1)
        lane_value = lane.astype(jnp.float32)
        hit = lane_value == block
        column = jnp.sum(
            jnp.where(iota((4, 16), 1) == member_slot[...], generator[...], 0.0), axis=1, keepdims=True
        )
        spread = jnp.sum(jnp.where(iota((4, 16), 0) == iota((4, 16), 1) // 4, column, 0.0), axis=0, keepdims=True)
        scale = jnp.sum(jnp.where(hit, spread, 0.0), axis=1, keepdims=True)
        quarter = jnp.sum(
            jnp.where(hit, lax.rem(lane, 4).astype(jnp.float32), 0.0), axis=1, keepdims=True
        )
        _, _, row_in = parts((64, 16))
        select.ref[...] = jnp.where(lane_value == quarter * 4.0 + row_in, scale, 0.0)

    def load_rest():
        for c in range(2, GRAD_SLOTS - 1):
            load(wide, c).start()
        for copy in given:
            copy.start()
        for c in range(NARROW_STEPS):
            load(narrow, c).start()
        selector()

    load(wide, 0).start()
    barrier = pltpu.get_barrier_semaphore()
    near = (XP, XM, ZP, ZM, YN, YH, CORE)
    for to in near:
        pl.semaphore_signal(barrier, inc=1, device_id=where[to], device_id_type=MESH)
    fill_wide(0)
    load(wide, 1).start()
    pl.semaphore_wait(barrier, len(near))

    first, wide_last, last = WIDE_STEPS, WIDE_STEPS - 1, NARROW_STEPS - 1
    turn = (
        (wide0, 0, wide_last),
        (narrow0, first, first + last),
        (wide1, 1, wide_last + 1),
        (wide4, 4, wide_last + 4),
        (wide3, 3, wide_last + 3),
        (wide2, 2, wide_last + 2),
        (wide1_side, 1, wide_last + 1),
        (narrow1, first + 1, first + 1 + last),
        (wide2_side, 2, wide_last + 2),
        (narrow2, first + 2, first + 2 + last),
        (wide3_side, 3, wide_last + 3),
        (narrow3, first + 3, first + 3 + last),
        (wide4_side, 4, wide_last + 4),
        (wide5, 5, wide_last + 5),
        (narrow4, first + 3, first + 3 + last),
        (wide7, 6, wide_last + 5),
        (narrow5, first + 4, first + 4 + last),
        (wide8, 7, wide_last + 6),
        (wide_end, wide_last + 6, wide_last + 6),
        (fill_wide, -1, wide_last - 1),
        (fill_narrow, first - 1, first - 1 + last),
        (wide6, 5, wide_last + 5),
    )
    turns = 1 + max(end for _, _, end in turn)

    def step(t, carry):
        for stage, begin, end in turn:

            @pl.when((t >= begin) & (t <= end))
            def _(stage=stage, begin=begin):
                stage(t - begin)

        @pl.when(t == 0)
        def _():
            load_rest()

        @pl.when((t > 0) & (t + GRAD_SLOTS - 2 < WIDE_STEPS))
        def _():
            load(wide, t + GRAD_SLOTS - 2).start()

        return carry

    lax.fori_loop(0, turns, step, 0)


def finish(count, *refs):
    given, outs, held = refs[:count], refs[count : 2 * count], refs[2 * count : 3 * count]
    sem = refs[3 * count]
    parts = []
    for at in range(count):
        pieces = 4 if given[at].shape[1] % 16 == 0 else 1
        columns = given[at].shape[2] // pieces
        for piece in range(pieces):
            part = (slice(None), slice(None), pl.ds(piece * columns, columns))
            parts.append(
                (
                    pltpu.make_async_copy(given[at].at[part], held[at].at[part], sem.at[0, at, piece]),
                    pltpu.make_async_copy(held[at].at[part], outs[at].at[part], sem.at[1, at, piece]),
                )
            )
    for read, _ in parts:
        read.start()
    for read, write in parts:
        read.wait()
        write.start()
    for _, write in parts:
        write.wait()


def shards(grads, master, moment_one, moment_two, generator, member_slot, holder):
    planned = plan()
    anywhere = pl.BlockSpec(memory_space=pl.ANY)
    vmem = pl.BlockSpec(memory_space=pltpu.VMEM)
    state = jax.ShapeDtypeStruct(master.shape, jnp.float32)
    made = (state, state, state, jax.ShapeDtypeStruct((1, 4, D), jnp.float32))
    results = pl.pallas_call(
        functools.partial(kernel, planned),
        out_shape=made,
        in_specs=[anywhere] * 4 + [vmem] * 3,
        out_specs=(anywhere, anywhere, anywhere, vmem),
        scratch_shapes=[part.spec for part in planned[0]],
        name="adam_parity",
        compiler_params=pltpu.CompilerParams(
            collective_id=0, has_side_effects=True, vmem_limit_bytes=63 * 2**20
        ),
    )(grads, master, moment_one, moment_two, generator, member_slot, holder.T)
    return pl.pallas_call(
        functools.partial(finish, 4),
        out_shape=made,
        in_specs=[anywhere] * 4,
        out_specs=(anywhere,) * 4,
        scratch_shapes=[pltpu.VMEM(part.shape, part.dtype) for part in made] + [pltpu.SemaphoreType.DMA((2, 4, 4))],
        name="write_out",
        compiler_params=pltpu.CompilerParams(vmem_limit_bytes=63 * 2**20),
    )(*results)


def solution(mesh):
    state = P("code", "dp", None)
    return jax.shard_map(
        shards,
        mesh=mesh,
        in_specs=(P("dp", "code", None, None), state, state, state, P(), P("dp", "code"), P()),
        out_specs=(state, state, state, state),
        check_vma=False,
    )
```
